32 devices in a mesh: groups: 2 (over x), seg: 16 (over z, y, core).
Axes of the slice: x: 2, y: 2, z: 4, core: 2. Of those that a mesh axis runs over, the one named last changes fastest.
Arguments:
- hidden: bfloat16 [1024, 28672], P(('groups', 'seg')), parts along dimension 0, may hold values from -6 to 6
- base_down_matrix: bfloat16 [28672, 8192], P('seg'), may hold values from -0.03125 to 0.03125
- adapter_shrink_blocks: bfloat16 [16, 28672, 128], P('seg'), may hold values from -0.03125 to 0.03125
- adapter_expand_blocks: bfloat16 [16, 128, 8192], P('seg'), may hold values from -0.5 to 0.5
- row_adapter_index: int32 [1024, 1], P(('groups', 'seg')), parts along dimension 0, may hold values from 0 to 15; in each aligned block of 32 rows (0 to 31, 32 to 63, ...) at most 2 rows name the same one
- adapter_storage_slot: int32 [16], replicated, may hold values from 0 to 15, each once
Outputs:
- output: bfloat16 [1024, 8192], P(('groups', 'seg')), parts along dimension 0
The draws below stay inside these ranges and needn't reach their ends.
There are 2 independent parts, one for each index of `groups`. The reference program is written for one: setup_inputs(seed, part) draws one part's arguments, and reference() takes and returns one part's arrays. A program takes and returns all parts, laid end to end along the dimension named above; an argument that names none is the same for every part. Nothing has to cross between parts.
Inputs may be any that keep to these rules, and one draw needn't show every extreme that they name: `row_adapter_index`: within the rows of one device no adapter is named more than 2 times, and in every draw some adapter is named exactly 2 times on some device. Each storage slot is used by exactly one adapter; adapter a's blocks are adapter_shrink_blocks[adapter_storage_slot[a]] and adapter_expand_blocks[adapter_storage_slot[a]].
All inputs are finite; a program needn't handle non-finite values.
Results may differ from the reference program's by a relative error of at most 0.005.
Values may be sent and summed in bfloat16 or wider, within the bound.
A program may use at most 192 MiB of HBM per device.

```python
import math
import jax
import jax.numpy as jnp
import numpy as np
from jax import lax

MODEL_WIDTH = 8192
HIDDEN_UNITS = 28672
ADAPTER_RANK = 128
MOST = 2
TOK_DEV = 32
TOKENS = 512
ADAPTER_COUNT = 16
N_SEG = 16


def levels(rng, extent, split, low, high):
    factor_of, own = 1.0, jax.random.fold_in(rng, 6)
    for dim, parts in split:
        heights = jnp.exp(jax.random.uniform(jax.random.fold_in(own, dim), (parts,), jnp.float32, low / len(split), high / len(split)))
        factor_of = factor_of * jnp.repeat(heights, extent[dim] // parts).reshape([-1 if axis == dim else 1 for axis in range(len(extent))])
    return factor_of


def routed_block(own_key, own, number, rows, amount, top, limit, lean):
    sequence = jax.random.permutation(own_key, amount)
    crowded, ordinary = shares(amount, rows * top, limit, lean, True), shares(amount, rows * top, limit, lean, False)
    places = jnp.arange(amount)

    def named(lengths, rotation):
        used = int((lengths > 0).sum())
        fixed = max(1, used // 4)
        passed = fixed + (places - fixed + rotation * (used - fixed)) % max(1, amount - fixed)
        return jnp.zeros((amount,), jnp.int32).at[sequence[jnp.where(places < fixed, places, passed)]].set(jnp.asarray(lengths, jnp.int32))

    lengths = jnp.where(number % 4 == 0, named(crowded, number // 4), named(ordinary, number - number // 4 - 1))
    mixed = jax.random.permutation(jax.random.fold_in(own, 3), amount)
    donor, taker = mixed[0:amount // 2 * 2:2], mixed[1:amount // 2 * 2:2]
    room = jnp.minimum(lengths[donor] - 1, limit - lengths[taker]) // 2
    room = jnp.where((donor == sequence[0]) | (taker == sequence[0]) | (lengths[taker] == 0), 0, jnp.maximum(room, 0))
    passed = jax.random.randint(jax.random.fold_in(own, 4), (amount // 2,), 0, 1 << 20) % (room + 1)
    lengths = lengths.at[donor].add(-passed).at[taker].add(passed)
    items = jnp.searchsorted(jnp.cumsum(lengths), jnp.arange(rows * top), side="right").astype(jnp.int32)
    table = items.reshape(top, rows).T
    table = table[jax.random.permutation(jax.random.fold_in(own, 1), rows)]
    rotation = jax.random.randint(jax.random.fold_in(own, 2), (rows, 1), 0, top)
    return jnp.take_along_axis(table, (jnp.arange(top)[None, :] + rotation) % top, axis=1)


def shares(number_of, total, limit, slope, full):
    loads = [(1 << 20) // math.isqrt(grade ** slope) + 1 for grade in range(1, number_of + 1)]
    largest = limit if full else min(limit, max(-(-total // number_of), total * loads[0] // sum(loads)))
    least = 1 if total - largest >= number_of - 1 else 0
    counts, rest = [largest] + [least] * (number_of - 1), total - largest - least * (number_of - 1)
    while rest > 0:
        movable = [i for i in range(1, number_of) if counts[i] < largest] or [i for i in range(1, number_of) if counts[i] < limit]
        mass, budget = sum([loads[i] for i in movable]), rest
        for i in movable:
            extra = min(limit - counts[i], max(1, budget * loads[i] // mass), rest)
            counts[i] = counts[i] + extra
            rest = rest - extra
    return np.array(counts)


def noise(rng, extent, scale, limit, pieces=(), kind=jnp.bfloat16):
    entries = jax.random.normal(rng, extent, jnp.float32) * scale
    if len(pieces) > 0:
        entries = levels(rng, extent, pieces, -0.22, 0.18) * entries
    return jnp.clip(entries, min=-limit, max=limit).astype(kind)


def setup_inputs(seed: int = 0, part: int = 0) -> dict:
    keys = jax.random.split(jax.random.key(seed), 7)
    part_keys = jax.random.split(jax.random.fold_in(keys[6], part), 7)
    hidden = noise(part_keys[0], (TOKENS, HIDDEN_UNITS), 1.0, 6.0, ((0, 16),))
    base_down_matrix = noise(keys[1], (HIDDEN_UNITS, MODEL_WIDTH), HIDDEN_UNITS ** -0.5, 0.03125, ((0, 16),))
    adapter_shrink_blocks = noise(keys[2], (ADAPTER_COUNT, HIDDEN_UNITS, ADAPTER_RANK), HIDDEN_UNITS ** -0.5, 0.03125, ((0, 16),))
    adapter_expand_blocks = noise(keys[3], (ADAPTER_COUNT, ADAPTER_RANK, MODEL_WIDTH), ADAPTER_RANK ** -0.5, 0.5, ((0, 16),))
    row_adapter_index_keys = jax.random.split(jax.random.fold_in(part_keys[4], 1), TOKENS // TOK_DEV)
    row_adapter_index_turns = jax.random.permutation(jax.random.fold_in(part_keys[4], 3), TOKENS // TOK_DEV)
    row_adapter_index = jax.vmap(lambda own, number: routed_block(jax.random.fold_in(part_keys[4], 2), own, number, TOK_DEV, ADAPTER_COUNT, 1, MOST, 2))(row_adapter_index_keys, row_adapter_index_turns).reshape((TOKENS, 1))
    adapter_storage_slot = jax.random.permutation(keys[5], ADAPTER_COUNT).astype(jnp.int32)
    return dict(hidden=hidden, base_down_matrix=base_down_matrix, adapter_shrink_blocks=adapter_shrink_blocks, adapter_expand_blocks=adapter_expand_blocks, row_adapter_index=row_adapter_index, adapter_storage_slot=adapter_storage_slot)


def reference(hidden, base_down_matrix, adapter_shrink_blocks, adapter_expand_blocks, row_adapter_index, adapter_storage_slot):
    base_sum = jnp.dot(hidden, base_down_matrix, preferred_element_type=jnp.float32)
    adapter_of = row_adapter_index[:, 0]
    capacity = MOST * N_SEG

    def add_adapter(summed, adapter):
        picked = jnp.nonzero(adapter_of == adapter, size=capacity, fill_value=TOKENS)[0].astype(jnp.int32)
        clipped = jnp.minimum(picked, TOKENS - 1)
        row_data = jnp.take(hidden, clipped, axis=0)
        row_storage_slot = adapter_storage_slot[adapter].astype(jnp.int32)
        shrink_output = lax.dynamic_index_in_dim(adapter_shrink_blocks, row_storage_slot, 0, keepdims=False)
        expand_output = lax.dynamic_index_in_dim(adapter_expand_blocks, row_storage_slot, 0, keepdims=False)
        shrunk = jnp.dot(row_data, shrink_output, preferred_element_type=jnp.float32).astype(jnp.bfloat16)
        update = jnp.dot(shrunk, expand_output, preferred_element_type=jnp.float32).astype(jnp.bfloat16)
        summed = summed.at[picked].add(update.astype(jnp.float32), mode="drop")
        return summed, None

    summed, _ = lax.scan(add_adapter, base_sum, jnp.arange(ADAPTER_COUNT, dtype=jnp.int32))
    return summed.astype(jnp.bfloat16)
```

```python
import functools

import jax
import jax.numpy as jnp
from jax import lax
from jax.experimental import pallas as pl
from jax.experimental.pallas import tpu as pltpu
from jax.sharding import PartitionSpec as P

MOST = 2
TILE = 16
PIECES = TILE // MOST
LANES = 128
SLOTS = 4
LAG = 2
MESH = pl.DeviceIdType.MESH


def reversed_bits(value, bits):
    return sum(((value >> b) & 1) << (bits - 1 - b) for b in range(bits))


def partner_of(me, offset, bits):
    for b in range(bits):
        if (offset >> b) & 1:
            me = me + (1 - 2 * ((me // (1 << b)) % 2)) * (1 << b)
    return me


def kernel(n, bits, chunk, rows, message_ref, hidden_ref, base_ref, shrink_ref, expand_ref, out_ref,
           features, messages, shrink, expand, base, spread, shrunk, *rest):
    keeps, sends, recvs = rest[:bits], rest[bits:2 * bits], rest[2 * bits:3 * bits]
    send_sems, recv_sems = rest[3 * bits:4 * bits], rest[4 * bits:5 * bits]
    base_sem, weight_sem, own_sem, message_send, message_recv, hidden_send, hidden_recv = rest[5 * bits:]
    me = lax.axis_index("seg")
    depth = base_ref.shape[0]
    steps = base_ref.shape[1] // chunk
    piece = messages.shape[1] - LANES
    slot_count = n * MOST

    def base_copy(i, slot):
        columns = pl.ds(pl.multiple_of(i * chunk, chunk), chunk)
        return pltpu.make_async_copy(base_ref.at[:, columns], base.at[slot], base_sem.at[slot])

    shrink_copy = pltpu.make_async_copy(shrink_ref.at[0], shrink, weight_sem.at[0])
    expand_copy = pltpu.make_async_copy(expand_ref.at[0], expand, weight_sem.at[1])
    own_message = pltpu.make_async_copy(
        message_ref.at[pl.ds(pl.multiple_of(me * TILE, TILE), TILE), :], messages.at[pl.ds(0, TILE), :], own_sem.at[0])
    own_hidden = pltpu.make_async_copy(
        hidden_ref.at[:, pl.ds(pl.multiple_of(me * depth, LANES), depth)], features.at[pl.ds(0, rows), :], own_sem.at[1])

    barrier = pltpu.get_barrier_semaphore()
    for k in range(1, n):
        pl.semaphore_signal(barrier, inc=1, device_id={"seg": partner_of(me, k, bits)}, device_id_type=MESH)
    shrink_copy.start()
    expand_copy.start()
    own_message.start()
    own_hidden.start()
    for i in range(SLOTS):
        base_copy(i, i).start()
    pl.semaphore_wait(barrier, n - 1)

    message_copies, hidden_copies = [], []
    for k in range(n - 1, 0, -1):
        to, place = partner_of(me, k, bits), reversed_bits(k, bits)
        message_copies.append(pltpu.make_async_remote_copy(
            src_ref=message_ref.at[pl.ds(pl.multiple_of(to * TILE, TILE), TILE), :],
            dst_ref=messages.at[pl.ds(place * TILE, TILE), :],
            send_sem=message_send.at[k], recv_sem=message_recv.at[k],
            device_id={"seg": to}, device_id_type=MESH))
        hidden_copies.append(pltpu.make_async_remote_copy(
            src_ref=hidden_ref.at[:, pl.ds(pl.multiple_of(to * depth, LANES), depth)],
            dst_ref=features.at[pl.ds(place * rows, rows), :],
            send_sem=hidden_send.at[k], recv_sem=hidden_recv.at[k],
            device_id={"seg": to}, device_id_type=MESH))
    for copy in message_copies:
        copy.start()
    for copy in hidden_copies:
        copy.start()

    shrink_copy.wait()
    expand_copy.wait()
    own_message.wait()
    for copy in message_copies:
        copy.wait()

    piece_of = lax.broadcasted_iota(jnp.int32, (slot_count * PIECES, LANES), 0) & (PIECES - 1)

    def shrink_piece(p, total):
        part = jnp.dot(messages[:, pl.ds(0, piece)], shrink[pl.ds(pl.multiple_of(p * piece, LANES), piece), :],
                       preferred_element_type=jnp.float32)
        return total + jnp.where(piece_of == p, part, 0.0)

    total = lax.fori_loop(0, PIECES, shrink_piece, jnp.zeros((slot_count * PIECES, LANES), jnp.float32))
    shrunk[...] = jnp.sum(total.reshape(slot_count, PIECES, LANES), axis=1).astype(jnp.bfloat16)
    tags = messages[:, pl.ds(piece, LANES)].astype(jnp.float32).reshape(slot_count, PIECES, LANES)
    tags = jnp.concatenate([jnp.max(tags, axis=1)] * (n * rows // LANES), axis=1)
    tags = jnp.where(
        lax.broadcasted_iota(jnp.int32, tags.shape, 0) // MOST == lax.broadcasted_iota(jnp.int32, tags.shape, 1) // rows,
        tags, 0.0)
    spread[...] = jnp.transpose(tags).astype(jnp.bfloat16)

    own_hidden.wait()
    for copy in hidden_copies:
        copy.wait()

    def sum_copy(stage, i):
        slot = i % SLOTS
        return pltpu.make_async_remote_copy(
            src_ref=sends[stage].at[slot], dst_ref=recvs[stage].at[i],
            send_sem=send_sems[stage].at[slot], recv_sem=recv_sems[stage].at[i],
            device_id={"seg": partner_of(me, 1 << stage, bits)}, device_id_type=MESH)

    def pass_on(stage, i, value):
        half = value.shape[0] // 2
        slot = i % SLOTS

        @pl.when(i >= SLOTS)
        def _():
            sum_copy(stage, i - SLOTS).wait_send()

        sends[stage][slot] = value[half:].astype(jnp.bfloat16)
        sum_copy(stage, i).start()
        keeps[stage][slot] = value[:half]

    def received(stage, i):
        sum_copy(stage, i).wait_recv()
        return keeps[stage][i % SLOTS] + recvs[stage][i].astype(jnp.float32)

    behind = [0] + [1 + LAG * s for s in range(bits)]

    def step(i, carry):
        @pl.when(i < steps)
        def _():
            slot = i % SLOTS
            base_copy(i, slot).wait()
            columns = pl.ds(pl.multiple_of(i * chunk, chunk), chunk)
            update = jnp.dot(shrunk[...], expand[:, columns], preferred_element_type=jnp.float32).astype(jnp.bfloat16)
            value = jnp.dot(features[...], base[slot], preferred_element_type=jnp.float32)
            value = value + jnp.dot(spread[...], update, preferred_element_type=jnp.float32)
            pass_on(0, i, value)

            @pl.when(i + SLOTS < steps)
            def _():
                base_copy(i + SLOTS, slot).start()

        for stage in range(1, bits + 1):
            j = i - behind[stage]

            @pl.when((j >= 0) & (j < steps))
            def _():
                value = received(stage - 1, j)
                if stage < bits:
                    pass_on(stage, j, value)
                else:
                    out_ref[:, pl.ds(pl.multiple_of(j * chunk, chunk), chunk)] = value.astype(out_ref.dtype)

        return carry

    lax.fori_loop(0, steps + behind[-1], step, 0)
    for stage in range(bits):
        for i in range(max(0, steps - SLOTS), steps):
            sum_copy(stage, i).wait_send()


def local(hidden, base_down_matrix, adapter_shrink_blocks, adapter_expand_blocks, row_adapter_index,
          adapter_storage_slot):
    n = lax.axis_size("seg")
    bits = n.bit_length() - 1
    rows, ff_width = hidden.shape
    depth, width = base_down_matrix.shape
    rank = adapter_shrink_blocks.shape[2]
    slot_count = n * MOST
    piece = ff_width // PIECES
    chunk = min(512, width // SLOTS)
    steps = width // chunk

    adapter_of = row_adapter_index[:, 0]
    table_size = adapter_storage_slot.shape[0]
    owner_of = jnp.sum(
        jnp.where(adapter_of[:, None] == jnp.arange(table_size, dtype=jnp.int32)[None, :],
                  adapter_storage_slot[None, :], 0), axis=1)
    row_index = jnp.arange(rows, dtype=jnp.int32)
    earlier = jnp.sum(
        ((adapter_of[:, None] == adapter_of[None, :]) & (row_index[None, :] < row_index[:, None])).astype(jnp.int32),
        axis=1)
    position = owner_of * MOST + earlier
    line = jnp.arange(slot_count * PIECES, dtype=jnp.int32)
    source = jnp.arange(PIECES * rows, dtype=jnp.int32)
    pick = (jnp.tile(position, PIECES)[None, :] == (line // PIECES)[:, None]) & (
        (source // rows)[None, :] == (line % PIECES)[:, None])
    pieces = hidden.reshape(rows, PIECES, piece).transpose(1, 0, 2).reshape(PIECES * rows, piece)
    tag = ((source % rows)[:, None] == (jnp.arange(LANES, dtype=jnp.int32) % rows)[None, :]).astype(jnp.bfloat16)
    message = jnp.dot(pick.astype(jnp.bfloat16), jnp.concatenate([pieces, tag], axis=1),
                      preferred_element_type=jnp.float32).astype(jnp.bfloat16)

    halves = [n * rows >> (s + 1) for s in range(bits)]
    anywhere = pl.BlockSpec(memory_space=pl.ANY)
    return pl.pallas_call(
        functools.partial(kernel, n, bits, chunk, rows),
        out_shape=jax.ShapeDtypeStruct((rows, width), jnp.bfloat16),
        in_specs=[anywhere] * 5,
        out_specs=pl.BlockSpec(memory_space=pltpu.VMEM),
        scratch_shapes=[
            pltpu.VMEM((n * rows, depth), jnp.bfloat16),
            pltpu.VMEM((n * TILE, piece + LANES), jnp.bfloat16),
            pltpu.VMEM((ff_width, rank), jnp.bfloat16),
            pltpu.VMEM((rank, width), jnp.bfloat16),
            pltpu.VMEM((SLOTS, depth, chunk), jnp.bfloat16),
            pltpu.VMEM((n * rows, slot_count), jnp.bfloat16),
            pltpu.VMEM((slot_count, rank), jnp.bfloat16),
            *[pltpu.VMEM((SLOTS, h, chunk), jnp.float32) for h in halves],
            *[pltpu.VMEM((SLOTS, h, chunk), jnp.bfloat16) for h in halves],
            *[pltpu.VMEM((steps, h, chunk), jnp.bfloat16) for h in halves],
            *[pltpu.SemaphoreType.DMA((SLOTS,)) for _ in halves],
            *[pltpu.SemaphoreType.DMA((steps,)) for _ in halves],
            pltpu.SemaphoreType.DMA((SLOTS,)),
            pltpu.SemaphoreType.DMA((2,)),
            pltpu.SemaphoreType.DMA((2,)),
            *[pltpu.SemaphoreType.DMA((n,)) for _ in range(4)],
        ],
        compiler_params=pltpu.CompilerParams(
            collective_id=0, has_side_effects=True, vmem_limit_bytes=58 * 1024 * 1024),
        cost_estimate=pl.CostEstimate(
            flops=2 * n * rows * depth * width, bytes_accessed=2 * depth * width, transcendentals=0),
    )(message, hidden, base_down_matrix, adapter_shrink_blocks, adapter_expand_blocks)


def solution(mesh):
    return jax.shard_map(
        local,
        mesh=mesh,
        in_specs=(
            P(("groups", "seg"), None),
            P("seg", None),
            P("seg", None, None),
            P("seg", None, None),
            P(("groups", "seg"), None),
            P(),
        ),
        out_specs=P(("groups", "seg"), None),
        check_vma=False,
    )
```

```python
import functools

import jax
import jax.numpy as jnp
from jax import lax
from jax.experimental import pallas as pl
from jax.experimental.pallas import tpu as pltpu
from jax.sharding import PartitionSpec as P

MOST = 2
TILE = 16
PIECES = TILE // MOST
LANES = 128
SLOTS = 4
LAG = 2
CHUNK = 512
FILL = 2
EARLY = False
AFTER = -4
MESH = pl.DeviceIdType.MESH


def reversed_bits(value, bits):
    return sum(((value >> b) & 1) << (bits - 1 - b) for b in range(bits))


def partner_of(me, offset, bits):
    for b in range(bits):
        if (offset >> b) & 1:
            me = me + (1 - 2 * ((me // (1 << b)) % 2)) * (1 << b)
    return me


def kernel(n, bits, chunk, rows, pick_ref, place_ref, hidden_ref, base_ref, shrink_ref, expand_ref, out_ref,
           features, pieces, outbox, messages, shrink, expand, base, updates, returned, base_rows, *rest):
    keeps, sends, recvs = rest[:bits], rest[bits:2 * bits], rest[2 * bits:3 * bits]
    send_sems, recv_sems = rest[3 * bits:4 * bits], rest[4 * bits:5 * bits]
    base_sem, weight_sem, own_sem, piece_sem = rest[5 * bits:5 * bits + 4]
    message_send, message_recv, hidden_send, hidden_recv, return_send, return_recv = rest[5 * bits + 4:]
    me = lax.axis_index("seg")
    depth = base_ref.shape[0]
    steps = base_ref.shape[1] // chunk
    piece = messages.shape[1]
    span = updates.shape[1]
    slot_count = n * MOST

    def base_copy(i, slot):
        columns = pl.ds(pl.multiple_of(i * chunk, chunk), chunk)
        return pltpu.make_async_copy(base_ref.at[:, columns], base.at[slot], base_sem.at[slot])

    weight_copies = []
    for p in range(PIECES):
        weight_copies.append(pltpu.make_async_copy(
            shrink_ref.at[0, pl.ds(p * piece, piece), :],
            shrink.at[pl.ds(p // 2 * piece, piece), pl.ds(p % 2 * LANES, LANES)], weight_sem.at[0, p]))
        weight_copies.append(pltpu.make_async_copy(
            expand_ref.at[0, :, pl.ds(p * span, span)], expand.at[pl.ds(p * LANES, LANES), :], weight_sem.at[1, p]))
    piece_copies = [
        pltpu.make_async_copy(hidden_ref.at[:, pl.ds(p * piece, piece)], pieces.at[pl.ds(p * rows, rows), :], piece_sem.at[p])
        for p in range(PIECES)]
    own_hidden = pltpu.make_async_copy(
        hidden_ref.at[:, pl.ds(pl.multiple_of(me * depth, LANES), depth)], features.at[pl.ds(0, rows), :], own_sem.at[0])

    barrier = pltpu.get_barrier_semaphore()
    for k in range(1, n):
        pl.semaphore_signal(barrier, inc=1, device_id={"seg": partner_of(me, k, bits)}, device_id_type=MESH)
    for copy in piece_copies:
        copy.start()
    own_hidden.start()
    pl.semaphore_wait(barrier, n - 1)

    message_copies, hidden_copies, return_copies = [], [], []
    for k in range(n - 1, 0, -1):
        to, place = partner_of(me, k, bits), reversed_bits(k, bits)
        theirs, mine = pl.ds(pl.multiple_of(to * TILE, TILE), TILE), pl.ds(pl.multiple_of(me * TILE, TILE), TILE)
        message_copies.append(pltpu.make_async_remote_copy(
            src_ref=outbox.at[theirs, :], dst_ref=messages.at[pl.ds(k * TILE, TILE), :],
            send_sem=message_send.at[k], recv_sem=message_recv.at[k],
            device_id={"seg": to}, device_id_type=MESH))
        return_copies.append(pltpu.make_async_remote_copy(
            src_ref=updates.at[pl.ds(k * TILE, TILE), :], dst_ref=returned.at[mine, :],
            send_sem=return_send.at[k], recv_sem=return_recv.at[k],
            device_id={"seg": to}, device_id_type=MESH))
        hidden_copies.append(pltpu.make_async_remote_copy(
            src_ref=hidden_ref.at[:, pl.ds(pl.multiple_of(to * depth, LANES), depth)],
            dst_ref=features.at[pl.ds(place * rows, rows), :],
            send_sem=hidden_send.at[k], recv_sem=hidden_recv.at[k],
            device_id={"seg": to}, device_id_type=MESH))
    for copy in hidden_copies:
        copy.start()
    for i in range(SLOTS):
        base_copy(i, i).start()
    for copy in weight_copies:
        copy.start()

    for copy in piece_copies:
        copy.wait()
    part = piece // FILL

    def fill(c, carry):
        columns = pl.ds(pl.multiple_of(c * part, LANES), part)
        outbox[:, columns] = jnp.dot(
            pick_ref[...], pieces[:, columns], preferred_element_type=jnp.float32).astype(jnp.bfloat16)
        return carry

    lax.fori_loop(0, FILL, fill, 0)
    messages[pl.ds(0, TILE), :] = outbox[pl.ds(pl.multiple_of(me * TILE, TILE), TILE), :]

    own_hidden.wait()
    if EARLY:
        for copy in message_copies:
            copy.start()
    for copy in hidden_copies:
        copy.wait()
    if not EARLY:
        for copy in message_copies:
            copy.start()

    def adapt():
        for copy in weight_copies:
            copy.wait()
        for copy in message_copies:
            copy.wait()
        lines = slot_count * PIECES

        def piece_and_lane(width):
            piece_of = lax.broadcasted_iota(jnp.int32, (lines, width), 0) & (PIECES - 1)
            return piece_of, lax.broadcasted_iota(jnp.int32, (lines, width), 1) // LANES

        def shrink_pair(q, total):
            term = jnp.dot(messages[...], shrink[pl.ds(pl.multiple_of(q * piece, LANES), piece), :],
                           preferred_element_type=jnp.float32)
            piece_of, lane = piece_and_lane(2 * LANES)
            return total + jnp.where(piece_of == 2 * q + lane, term, 0.0)

        total = lax.fori_loop(0, PIECES // 2, shrink_pair, jnp.zeros((lines, 2 * LANES), jnp.float32))
        total = total[:, :LANES] + total[:, LANES:]
        total = jnp.sum(total.reshape(slot_count, PIECES, LANES), axis=1, keepdims=True)
        shrunk = jnp.broadcast_to(total, (slot_count, PIECES, LANES)).reshape(lines, LANES)
        piece_of, lane = piece_and_lane(PIECES * LANES)
        shrunk = jnp.where(piece_of == lane, jnp.concatenate([shrunk] * PIECES, axis=1), 0.0).astype(jnp.bfloat16)
        updates[...] = jnp.dot(shrunk, expand[...], preferred_element_type=jnp.float32).astype(jnp.bfloat16)
        returned[pl.ds(pl.multiple_of(me * TILE, TILE), TILE), :] = updates[pl.ds(0, TILE), :]
        for copy in return_copies:
            copy.start()

    def sum_copy(stage, i):
        slot = i % SLOTS
        return pltpu.make_async_remote_copy(
            src_ref=sends[stage].at[slot], dst_ref=recvs[stage].at[i],
            send_sem=send_sems[stage].at[slot], recv_sem=recv_sems[stage].at[i],
            device_id={"seg": partner_of(me, 1 << stage, bits)}, device_id_type=MESH)

    def pass_on(stage, i, value):
        half = value.shape[0] // 2
        slot = i % SLOTS

        @pl.when(i >= SLOTS)
        def _():
            sum_copy(stage, i - SLOTS).wait_send()

        sends[stage][slot] = value[half:].astype(jnp.bfloat16)
        sum_copy(stage, i).start()
        keeps[stage][slot] = value[:half]

    def received(stage, i):
        sum_copy(stage, i).wait_recv()
        return keeps[stage][i % SLOTS] + recvs[stage][i].astype(jnp.float32)

    behind = [0] + [1 + LAG * s for s in range(bits)]

    def step(i, carry):
        @pl.when(i < steps)
        def _():
            slot = i % SLOTS
            base_copy(i, slot).wait()
            value = jnp.dot(features[...], base[slot], preferred_element_type=jnp.float32)
            pass_on(0, i, value)

            @pl.when(i + SLOTS < steps)
            def _():
                base_copy(i + SLOTS, slot).start()

        for stage in range(1, bits + 1):
            j = i - behind[stage]

            @pl.when((j >= 0) & (j < steps))
            def _():
                value = received(stage - 1, j)
                if stage < bits:
                    pass_on(stage, j, value)
                else:
                    base_rows[:, pl.ds(pl.multiple_of(j * chunk, chunk), chunk)] = value

        @pl.when(i == steps + AFTER)
        def _():
            adapt()

        return carry

    lax.fori_loop(0, steps + behind[-1], step, 0)
    for copy in return_copies:
        copy.wait()
    for p in range(PIECES):
        columns = pl.ds(p * span, span)
        update = jnp.dot(place_ref[pl.ds(p * rows, rows), :], returned[...], preferred_element_type=jnp.float32)
        out_ref[:, columns] = (base_rows[:, columns] + update).astype(out_ref.dtype)
    for stage in range(bits):
        for i in range(max(0, steps - SLOTS), steps):
            sum_copy(stage, i).wait_send()


def local(hidden, base_down_matrix, adapter_shrink_blocks, adapter_expand_blocks, row_adapter_index,
          adapter_storage_slot):
    n = lax.axis_size("seg")
    bits = n.bit_length() - 1
    rows, ff_width = hidden.shape
    depth, width = base_down_matrix.shape
    rank = adapter_shrink_blocks.shape[2]
    slot_count = n * MOST
    piece = ff_width // PIECES
    chunk = min(CHUNK, width // SLOTS)
    steps = width // chunk

    adapter_of = row_adapter_index[:, 0]
    table_size = adapter_storage_slot.shape[0]
    owner_of = jnp.sum(
        jnp.where(adapter_of[:, None] == jnp.arange(table_size, dtype=jnp.int32)[None, :],
                  adapter_storage_slot[None, :], 0), axis=1)
    row_index = jnp.arange(rows, dtype=jnp.int32)
    earlier = jnp.sum(
        ((adapter_of[:, None] == adapter_of[None, :]) & (row_index[None, :] < row_index[:, None])).astype(jnp.int32),
        axis=1)
    position = owner_of * MOST + earlier
    line = jnp.arange(slot_count * PIECES, dtype=jnp.int32)
    source = jnp.arange(PIECES * rows, dtype=jnp.int32)
    spots = jnp.tile(position, PIECES)
    pick = (spots[None, :] == (line // PIECES)[:, None]) & ((source // rows)[None, :] == (line % PIECES)[:, None])
    place = (spots[:, None] == (line // PIECES)[None, :]) & ((source // rows)[:, None] == (line % PIECES)[None, :])

    halves = [n * rows >> (s + 1) for s in range(bits)]
    anywhere = pl.BlockSpec(memory_space=pl.ANY)
    return pl.pallas_call(
        functools.partial(kernel, n, bits, chunk, rows),
        out_shape=jax.ShapeDtypeStruct((rows, width), jnp.bfloat16),
        in_specs=[pl.BlockSpec(memory_space=pltpu.VMEM)] * 2 + [anywhere] * 4,
        out_specs=pl.BlockSpec(memory_space=pltpu.VMEM),
        scratch_shapes=[
            pltpu.VMEM((n * rows, depth), jnp.bfloat16),
            pltpu.VMEM((PIECES * rows, piece), jnp.bfloat16),
            pltpu.VMEM((n * TILE, piece), jnp.bfloat16),
            pltpu.VMEM((n * TILE, piece), jnp.bfloat16),
            pltpu.VMEM((ff_width // 2, 2 * rank), jnp.bfloat16),
            pltpu.VMEM((PIECES * rank, width // PIECES), jnp.bfloat16),
            pltpu.VMEM((SLOTS, depth, chunk), jnp.bfloat16),
            pltpu.VMEM((n * TILE, width // PIECES), jnp.bfloat16),
            pltpu.VMEM((n * TILE, width // PIECES), jnp.bfloat16),
            pltpu.VMEM((rows, width), jnp.float32),
            *[pltpu.VMEM((SLOTS, h, chunk), jnp.float32) for h in halves],
            *[pltpu.VMEM((SLOTS, h, chunk), jnp.bfloat16) for h in halves],
            *[pltpu.VMEM((steps, h, chunk), jnp.bfloat16) for h in halves],
            *[pltpu.SemaphoreType.DMA((SLOTS,)) for _ in halves],
            *[pltpu.SemaphoreType.DMA((steps,)) for _ in halves],
            pltpu.SemaphoreType.DMA((SLOTS,)),
            pltpu.SemaphoreType.DMA((2, PIECES)),
            pltpu.SemaphoreType.DMA((1,)),
            pltpu.SemaphoreType.DMA((PIECES,)),
            *[pltpu.SemaphoreType.DMA((n,)) for _ in range(6)],
        ],
        compiler_params=pltpu.CompilerParams(
            collective_id=0, has_side_effects=True, vmem_limit_bytes=58 * 1024 * 1024),
        cost_estimate=pl.CostEstimate(
            flops=2 * n * rows * depth * width, bytes_accessed=2 * depth * width, transcendentals=0),
    )(pick.astype(jnp.bfloat16), place.astype(jnp.bfloat16), hidden, base_down_matrix, adapter_shrink_blocks, adapter_expand_blocks)


def solution(mesh):
    return jax.shard_map(
        local,
        mesh=mesh,
        in_specs=(
            P(("groups", "seg"), None),
            P("seg", None),
            P("seg", None, None),
            P("seg", None, None),
            P(("groups", "seg"), None),
            P(),
        ),
        out_specs=P(("groups", "seg"), None),
        check_vma=False,
    )
```
